32 devices in a mesh: dp: 4 (over y, x), fsdp: 8 (over z, core).
Axes of the slice: x: 2, y: 2, z: 4, core: 2. Of those that a mesh axis runs over, the one named last changes fastest.
Arguments:
- latents: bfloat16 [32, 256, 768], P(('dp', 'fsdp')), may hold values from -6 to 6
- conditioning: bfloat16 [32, 768], P(('dp', 'fsdp')), may hold values from -6 to 6
- cotangent: bfloat16 [32, 256, 768], P(('dp', 'fsdp')), may hold values from -6 to 6
- latent_count: int32 [32], P(('dp', 'fsdp')), may hold values from 0 to 1, as said below
- ada_weight: bfloat16 [768, 4608], P('dp', 'fsdp'), may hold values from -0.21875 to 0.21875
- ada_bias: bfloat16 [4608], P('fsdp'), may hold values from -3 to 3
- qkv_weight: bfloat16 [768, 2304], P('dp', 'fsdp'), may hold values from -0.21875 to 0.21875
- qv_bias: bfloat16 [1536], P('fsdp'), may hold values from -3 to 3
- proj_weight: bfloat16 [768, 768], P('dp', 'fsdp'), may hold values from -0.875 to 0.875
- proj_bias: bfloat16 [768], P('fsdp'), may hold values from -3 to 3
- fc1_weight: bfloat16 [768, 3072], P('dp', 'fsdp'), may hold values from -0.21875 to 0.21875
- fc1_bias: bfloat16 [3072], P('fsdp'), may hold values from -3 to 3
- fc2_weight: bfloat16 [3072, 768], P('dp', 'fsdp'), may hold values from -0.109375 to 0.109375
- fc2_bias: bfloat16 [768], P('fsdp'), may hold values from -3 to 3
Outputs:
- block_out: bfloat16 [32, 256, 768], P(('dp', 'fsdp'))
- latents_grad: bfloat16 [32, 256, 768], P(('dp', 'fsdp'))
- conditioning_grad: float32 [32, 768], P(('dp', 'fsdp'))
- ada_weight_grad: float32 [768, 4608], P('dp', 'fsdp')
- ada_bias_grad: float32 [4608], P('fsdp')
- qkv_weight_grad: float32 [768, 2304], P('dp', 'fsdp')
- qv_bias_grad: float32 [1536], P('fsdp')
- proj_weight_grad: float32 [768, 768], P('dp', 'fsdp')
- proj_bias_grad: float32 [768], P('fsdp')
- fc1_weight_grad: float32 [768, 3072], P('dp', 'fsdp')
- fc1_bias_grad: float32 [3072], P('fsdp')
- fc2_weight_grad: float32 [3072, 768], P('dp', 'fsdp')
- fc2_bias_grad: float32 [768], P('fsdp')
The draws below stay inside these ranges and needn't reach their ends.
Inputs may be any that keep to these rules, and one draw needn't show every extreme that they name: `latent_count`: exactly 8 slots hold no latent.
All inputs are finite; a program needn't handle non-finite values.
Results may differ from the reference program's by a relative error of at most 0.015.
The reference program's roundings to bfloat16 on the way count: a program that leaves them out, or rounds other values in their place, can miss the bound.
Values may be sent and summed in bfloat16 or wider, within the bound.
A program may use at most 128 MiB of HBM per device.

```python
import math
import jax
import jax.numpy as jnp
from jax import lax

D = 768
HEADS = 12
FF = 3072
SEQ = 256
LATENTS = 32


def draw_latent_count(key, part):
    shuffled = jax.random.permutation(jax.random.fold_in(key, 11), LATENTS)
    return (shuffled >= LATENTS // 4).astype(jnp.int32)


def block_scale(stream_key, dims, shards, least, top_value):
    def one(position, blocks):
        heights = jax.random.uniform(jax.random.fold_in(jax.random.fold_in(stream_key, 6), position), (blocks,), jnp.float32, least / len(shards), top_value / len(shards))
        return jnp.repeat(jnp.exp(heights), dims[position] // blocks).reshape((-1,) + (1,) * (len(dims) - position - 1))

    gain = one(*shards[0])
    for cut in shards[1:]:
        gain = gain * one(*cut)
    return gain


def bell_draw(rng, shape, scale, reach, cuts=(), held_as=jnp.bfloat16):
    array = scale * jax.random.normal(rng, shape, jnp.float32)
    if cuts:
        array = array * block_scale(rng, shape, cuts, -0.22, 0.18)
    return jnp.clip(array, -reach, reach).astype(held_as)


def setup_inputs(seed: int = 0) -> dict:
    splits = jax.random.split(jax.random.key(seed), 15)
    latents = bell_draw(splits[0], (LATENTS, SEQ, D), 1.0, 6.0, ((0, 32),))
    conditioning = bell_draw(splits[1], (LATENTS, D), 1.0, 6.0, ((0, 32),))
    cotangent = bell_draw(splits[2], (LATENTS, SEQ, D), 1.0, 6.0, ((0, 32),))
    latent_count = draw_latent_count(jax.random.fold_in(splits[14], 71), 0)
    ada_weight = bell_draw(splits[4], (D, 6 * D), D ** -0.5, 0.21875, ((0, 4), (1, 8)))
    ada_bias = bell_draw(splits[5], (6 * D,), 0.5, 3.0, ((0, 8),))
    qkv_weight = bell_draw(splits[6], (D, 3 * D), D ** -0.5, 0.21875, ((0, 4), (1, 8)))
    qv_bias = bell_draw(splits[7], (2 * D,), 0.5, 3.0, ((0, 8),))
    proj_weight = bell_draw(splits[8], (D, D), (D // 16) ** -0.5, 0.875, ((0, 4), (1, 8)))
    proj_bias = bell_draw(splits[9], (D,), 0.5, 3.0, ((0, 8),))
    fc1_weight = bell_draw(splits[10], (D, FF), D ** -0.5, 0.21875, ((0, 4), (1, 8)))
    fc1_bias = bell_draw(splits[11], (FF,), 0.5, 3.0, ((0, 8),))
    fc2_weight = bell_draw(splits[12], (FF, D), FF ** -0.5, 0.109375, ((0, 4), (1, 8)))
    fc2_bias = bell_draw(splits[13], (D,), 0.5, 3.0, ((0, 8),))
    return dict(latents=latents, conditioning=conditioning, cotangent=cotangent, latent_count=latent_count, ada_weight=ada_weight, ada_bias=ada_bias, qkv_weight=qkv_weight, qv_bias=qv_bias, proj_weight=proj_weight, proj_bias=proj_bias, fc1_weight=fc1_weight, fc1_bias=fc1_bias, fc2_weight=fc2_weight, fc2_bias=fc2_bias)


@jax.custom_vjp
def low(v):
    return lax.optimization_barrier(v.astype(jnp.bfloat16)).astype(jnp.float32)

@jax.custom_vjp
def low_back(v):
    return v

def low_keep(v):
    return (low(v), None)

def low_pass(kept, grad):
    return (grad,)

def back_keep(v):
    return (v, None)

def back_low(kept, grad):
    return (low(grad),)
low.defvjp(low_keep, low_pass)
low_back.defvjp(back_keep, back_low)
highest = lax.Precision.HIGHEST

def normalize(values):
    center = lax.optimization_barrier(jnp.mean(values, axis=-1, keepdims=True))
    spread = lax.optimization_barrier(jnp.mean(jnp.square(values - center), axis=-1, keepdims=True))
    return (values - center) * lax.rsqrt(spread + 1e-06)

def forward(latent_rows, cond_rows, live_rows, params):
    ada_weight, ada_bias, qkv_weight, qv_bias, proj_weight, proj_bias, fc1_weight, fc1_bias, fc2_weight, fc2_bias = params
    group_count, length, model_width = latent_rows.shape
    head_size = model_width // HEADS
    cond_act = low(jax.nn.silu(cond_rows))
    modulation = jnp.dot(cond_act, ada_weight, precision=highest) + ada_bias
    pieces = [segment[:, None, :] for segment in jnp.split(modulation, 6, axis=-1)]
    shift_one, scale_one, gate_one, shift_two, scale_two, gate_two = pieces
    hidden_one = low(normalize(latent_rows) * (1.0 + scale_one) + shift_one)
    qkv_bias = jnp.concatenate([qv_bias[:model_width], jnp.zeros((model_width,), jnp.float32), qv_bias[model_width:]])
    projected = low(low_back(jnp.einsum('gsd,de->gse', hidden_one, qkv_weight, precision=highest) + qkv_bias))
    queries, key_rows, values = [segment.reshape(group_count, length, HEADS, head_size) for segment in jnp.split(projected, 3, axis=-1)]
    scores = low_back(jnp.einsum('gqhe,gkhe->ghqk', queries, key_rows, precision=highest) * head_size ** (-0.5))
    row_max = lax.optimization_barrier(jnp.max(scores, axis=-1, keepdims=True))
    shifted = jnp.exp(scores - row_max)
    probability = low(shifted / lax.optimization_barrier(jnp.sum(shifted, axis=-1, keepdims=True)))
    attended = jnp.einsum('ghqk,gkhe->gqhe', probability, values, precision=highest).reshape(group_count, length, model_width)
    attended = low(low_back(attended))
    branch = low_back(jnp.einsum('gsd,de->gse', attended, proj_weight, precision=highest) + proj_bias)
    middle = latent_rows + gate_one * branch
    hidden_two = low(normalize(middle) * (1.0 + scale_two) + shift_two)
    pre_gelu = low_back(jnp.einsum('gsd,df->gsf', hidden_two, fc1_weight, precision=highest) + fc1_bias)
    activated = low(jax.nn.gelu(pre_gelu, approximate=True))
    mlp_out = low_back(jnp.einsum('gsf,fd->gsd', activated, fc2_weight, precision=highest) + fc2_bias)
    return (middle + gate_two * mlp_out) * live_rows[:, None, None]

def reference(latents, conditioning, cotangent, latent_count, ada_weight, ada_bias, qkv_weight, qv_bias, proj_weight, proj_bias, fc1_weight, fc1_bias, fc2_weight, fc2_bias):
    params = tuple((tensor.astype(jnp.float32) for tensor in (ada_weight, ada_bias, qkv_weight, qv_bias, proj_weight, proj_bias, fc1_weight, fc1_bias, fc2_weight, fc2_bias)))
    group_size = math.gcd(LATENTS, 16)
    rounds = LATENTS // group_size
    stacked = (latents.astype(jnp.float32).reshape(rounds, group_size, SEQ, D), conditioning.astype(jnp.float32).reshape(rounds, group_size, D), cotangent.astype(jnp.float32).reshape(rounds, group_size, SEQ, D), latent_count.astype(jnp.float32).reshape(rounds, group_size))

    def accumulate(totals, inputs):
        latent_rows, cond_rows, grad_rows, live_rows = inputs

        def run_layer(rows_in, cond_in, weights_in):
            return forward(rows_in, cond_in, live_rows, weights_in)
        result, pullback = jax.vjp(run_layer, latent_rows, cond_rows, params)
        latent_grad, cond_grad, param_grads = pullback(grad_rows)
        totals = jax.tree.map(lambda earlier, update: earlier + update, totals, param_grads)
        return (totals, (result.astype(jnp.bfloat16), latent_grad.astype(jnp.bfloat16), cond_grad))
    initial = jax.tree.map(jnp.zeros_like, params)
    totals, (outputs, latent_grads, cond_grads) = lax.scan(accumulate, initial, stacked)
    return (outputs.reshape(LATENTS, SEQ, D), latent_grads.reshape(LATENTS, SEQ, D), cond_grads.reshape(LATENTS, D), totals[0], totals[1], totals[2], totals[3], totals[4], totals[5], totals[6], totals[7], totals[8], totals[9])
```

```python
import functools
import jax
import jax.numpy as jnp
from jax import lax
from jax.sharding import PartitionSpec as P
from jax.experimental import pallas as pl
from jax.experimental.pallas import tpu as pltpu

MESH_IDS = pl.DeviceIdType.MESH
D = 768
HEADS = 12
HEAD = 64
FF = 3072

highest = lax.Precision.HIGHEST
bfloat = jnp.bfloat16


def place(dp_index, z_index, core):
    return (dp_index, z_index * 2 + core)


def z_order(size):
    steps = [0]
    for distance in range(1, size // 2 + 1):
        steps.append(distance)
        if size - distance != distance:
            steps.append(size - distance)
    return steps


def enter_barrier(partners):
    barrier = pltpu.get_barrier_semaphore()
    for partner in partners:
        pl.semaphore_signal(barrier, inc=1, device_id=partner, device_id_type=MESH_IDS)
    pl.semaphore_wait(barrier, len(partners))


def positions(rows, depth):
    dp = lax.axis_index("dp")
    column = lax.axis_index("fsdp")
    z, core = column // 2, column % 2
    others = [(dp ^ 1), (dp ^ 2)] if rows == 4 else [(dp + step) % rows for step in range(1, rows)]
    partners = [place(dp, z, 1 - core)]
    partners += [place(other, z, core) for other in others]
    partners += [place(dp, (z + step) % depth, core) for step in z_order(depth)[1:]]
    return dp, z, core, others, partners


def gather_kernel(rows, depth, shard, out, own_sem, send_sems, recv_sems):
    dp, z, core, others, partners = positions(rows, depth)
    height = shard.shape[0]
    half = height // 2
    sibling = place(dp, z, 1 - core)
    enter_barrier(partners)
    sends = []

    def send(source, line, row, part, target):
        destination, origin = out.at[line, row], source
        if part is not None and rows == 4:
            if part[1]:
                destination = destination.at[pl.ds(part[0] * half, half)]
                origin = source.at[pl.ds(part[0] * half, half)]
        slot = part[0] if part is not None else 0
        copy = pltpu.make_async_remote_copy(
            src_ref=origin,
            dst_ref=destination,
            send_sem=send_sems.at[len(sends)],
            recv_sem=recv_sems.at[slot, line, row],
            device_id=target,
            device_id_type=MESH_IDS,
        )
        copy.start()
        sends.append(copy)

    def arrive(line, row, part=None):
        destination = out.at[line, row]
        slot = 0
        if part is not None:
            slot = part
            destination = destination.at[pl.ds(part * half, half)]
        pltpu.make_async_remote_copy(
            src_ref=destination,
            dst_ref=destination,
            send_sem=send_sems.at[0],
            recv_sem=recv_sems.at[slot, line, row],
            device_id=sibling,
            device_id_type=MESH_IDS,
        ).wait_recv()

    own = z * 2 + core
    steps = z_order(depth)
    lines = [((z - step) % depth) * 2 + core for step in steps]
    for other in others:
        send(shard, own, dp, None, place(other, z, core))
    for step in steps[1:]:
        send(shard, own, dp, None, place(dp, (z + step) % depth, core))
    send(shard, own, dp, None, sibling)
    keep = pltpu.make_async_copy(shard, out.at[own, dp], own_sem)
    keep.start()
    for turn in range(depth + 2):
        if 0 < turn < depth:
            line = lines[turn]
            arrive(line, dp)
            for other in others:
                send(out.at[line, dp], line, dp, None, place(other, z, core))
            send(out.at[line, dp], line, dp, None, sibling)
        if 1 <= turn <= depth:
            line = lines[turn - 1]
            for position, other in enumerate(others):
                arrive(line, other)
                if rows == 4:
                    send(out.at[line, other], line, other, (position, True), place(others[1 - position], z, core))
                send(out.at[line, other], line, other, None, sibling)
        if turn >= 2 and rows == 4:
            line = lines[turn - 2]
            arrive(line, dp ^ 3, 0)
            arrive(line, dp ^ 3, 1)
            send(out.at[line, dp ^ 3], line, dp ^ 3, None, sibling)
    for line in lines:
        for row in range(rows):
            arrive(line + 1 - 2 * core, (dp + row) % rows)
    keep.wait()
    for copy in sends:
        copy.wait_send()


def gather_shards(shard, rows, columns):
    depth = columns // 2
    count = (depth - 1) + depth * rows + depth * (rows - 1) + (2 * depth if rows == 4 else 0)
    return pl.pallas_call(
        functools.partial(gather_kernel, rows, depth),
        out_shape=jax.ShapeDtypeStruct((columns, rows) + shard.shape, shard.dtype),
        in_specs=[pl.BlockSpec(memory_space=pl.ANY)],
        out_specs=pl.BlockSpec(memory_space=pl.ANY),
        scratch_shapes=[
            pltpu.SemaphoreType.DMA,
            pltpu.SemaphoreType.DMA((count,)),
            pltpu.SemaphoreType.DMA((2, columns, rows)),
        ],
        compiler_params=pltpu.CompilerParams(collective_id=0, has_side_effects=True),
        name="gather_shards",
    )(shard)


def scatter_kernel(
    rows, depth, grads, out, held, pair, plane, cross, along,
    load_sems, pair_send, pair_recv, plane_send, plane_recv, cross_send, cross_recv, along_send, along_recv,
):
    dp, z, core, others, partners = positions(rows, depth)
    height = out.shape[0]
    half = height // 2
    chunk = 48
    sibling = place(dp, z, 1 - core)
    targets = [dp ^ 3, dp ^ 1, dp ^ 2, dp] if rows == 4 else others + [dp]
    steps = z_order(depth)[::-1]
    enter_barrier(partners)
    waits = []

    def remote(source, destination, send_sem, recv_sem, target):
        return pltpu.make_async_remote_copy(
            src_ref=source, dst_ref=destination, send_sem=send_sem, recv_sem=recv_sem,
            device_id=target, device_id_type=MESH_IDS,
        )

    def start(copy):
        copy.start()
        waits.append(copy)
        return copy

    def add(first, others_in, length, target):
        @pl.loop(0, length // chunk)
        def _(index):
            piece = pl.ds(pl.multiple_of(index * chunk, chunk), chunk)
            total = first[piece, :].astype(jnp.float32)
            for other in others_in:
                total = total + other[piece, :].astype(jnp.float32)
            target[piece, :] = total.astype(target.dtype)

    lines = [(z + step) % depth for step in steps]
    pairs, loads = {}, {}
    for turn, line in enumerate(lines):
        for slot, target in enumerate(targets):
            pairs[turn, slot] = start(remote(
                grads.at[line * 2 + 1 - core, target], pair.at[turn, slot],
                pair_send.at[turn, slot], pair_recv.at[turn, slot], sibling))
            loads[turn, slot] = pltpu.make_async_copy(
                grads.at[line * 2 + core, target], held.at[turn, slot], load_sems.at[turn, slot])
            loads[turn, slot].start()
    last = len(targets) - 1
    planes, crosses, alongs = {}, {}, {}
    for turn in range(depth + 2):
        if turn < depth:
            for slot in range(len(targets)):
                loads[turn, slot].wait()
                pairs[turn, slot].wait_recv()
                here = held.at[turn, slot]
                add(here, [pair.at[turn, slot]], height, here)
                if rows == 4 and slot == 0:
                    for position in range(2):
                        part = pl.ds((1 - position) * half, half)
                        crosses[turn, position] = start(remote(
                            held.at[turn, 0, part], cross.at[turn, position],
                            cross_send.at[turn, position], cross_recv.at[turn, position],
                            place(others[position], z, core)))
                if rows != 4 and slot < last:
                    planes[turn, slot] = start(remote(
                        here, plane.at[turn, slot], plane_send.at[turn, slot],
                        plane_recv.at[turn, slot], place(targets[slot], z, core)))
        if rows == 4 and 1 <= turn <= depth:
            now = turn - 1
            for position in range(2):
                crosses[now, 1 - position].wait_recv()
                part = held.at[now, 1 + position, pl.ds(position * half, half)]
                add(part, [cross.at[now, 1 - position]], half, part)
                planes[now, position] = start(remote(
                    held.at[now, 1 + position], plane.at[now, position],
                    plane_send.at[now, position], plane_recv.at[now, position],
                    place(others[position], z, core)))
        if turn >= 2:
            now = turn - 2
            for slot in range(len(others)):
                planes[now, slot].wait_recv()
            here = held.at[now, last]
            add(here, [plane.at[now, slot] for slot in range(len(others))], height, here)
            if now < depth - 1:
                alongs[now] = start(remote(
                    here, along.at[now], along_send.at[now], along_recv.at[now],
                    place(dp, lines[now], core)))
    for now in range(depth - 1):
        alongs[now].wait_recv()
    add(held.at[depth - 1, last], [along.at[now] for now in range(depth - 1)], height, out)
    for copy in waits:
        copy.wait_send()


def scatter_shards(grads):
    columns, rows, height, width = grads.shape
    depth = columns // 2
    peers = 2 if rows == 4 else rows - 1
    half = height // 2 if rows == 4 else 16
    dma = pltpu.SemaphoreType.DMA
    kind = grads.dtype
    return pl.pallas_call(
        functools.partial(scatter_kernel, rows, depth),
        out_shape=jax.ShapeDtypeStruct((height, width), jnp.float32),
        in_specs=[pl.BlockSpec(memory_space=pl.ANY)],
        out_specs=pl.BlockSpec(memory_space=pltpu.VMEM),
        scratch_shapes=[
            pltpu.VMEM((depth, rows, height, width), kind),
            pltpu.VMEM((depth, rows, height, width), kind),
            pltpu.VMEM((depth, peers, height, width), kind),
            pltpu.VMEM((depth, 2, half, width), kind),
            pltpu.VMEM((depth - 1, height, width), kind),
            dma((depth, rows)), dma((depth, rows)), dma((depth, rows)),
            dma((depth, peers)), dma((depth, peers)),
            dma((depth, 2)), dma((depth, 2)),
            dma((depth - 1,)), dma((depth - 1,)),
        ],
        compiler_params=pltpu.CompilerParams(
            collective_id=1, has_side_effects=True, vmem_limit_bytes=50 * 2**20),
        name="scatter_shards",
    )(grads)


def normalize_rows(values):
    center = jnp.mean(values, axis=-1, keepdims=True)
    spread = jnp.mean(jnp.square(values - center), axis=-1, keepdims=True)
    inverse = lax.rsqrt(spread + 1e-06)
    return ((values - center) * inverse, inverse)


def norm_backward(grad_normed, normed, inverse):
    centered = grad_normed - jnp.mean(grad_normed, axis=-1, keepdims=True)
    return inverse * (centered - normed * jnp.mean(grad_normed * normed, axis=-1, keepdims=True))


def contract_rows(left_rows, right_rows):
    return lax.dot_general(
        left_rows, right_rows, (((0,), (0,)), ((), ())), preferred_element_type=jnp.float32
    )


def contract_exact(left_rows, right_rows):
    return lax.dot_general(left_rows, right_rows, (((0,), (0,)), ((), ())), precision=highest)


def against_weight(grad_rows, weight):
    return lax.dot_general(
        grad_rows, weight, (((1,), (1,)), ((), ())), preferred_element_type=jnp.float32
    )


def layer(latent_rows, cond_act, live, cot_rows, modulation, weights, biases):
    qkv_weight, proj_weight, fc1_weight, fc2_weight = weights
    qv_bias, proj_bias, fc1_bias, fc2_bias = biases
    length = latent_rows.shape[0]
    rows_wide = latent_rows.astype(jnp.float32)
    shift_one, scale_one, gate_one, shift_two, scale_two, gate_two = jnp.split(
        modulation, 6, axis=-1
    )
    normed_one, inverse_one = normalize_rows(rows_wide)
    hidden_one = (normed_one * (1.0 + scale_one) + shift_one).astype(bfloat)
    qkv_bias = jnp.concatenate([qv_bias[:D], jnp.zeros((D,), jnp.float32), qv_bias[D:]])
    projected = (
        jnp.dot(hidden_one, qkv_weight, preferred_element_type=jnp.float32) + qkv_bias
    ).astype(bfloat)
    queries = projected[:, :D].reshape(length, HEADS, HEAD)
    key_rows = projected[:, D : 2 * D].reshape(length, HEADS, HEAD)
    values = projected[:, 2 * D :].reshape(length, HEADS, HEAD)
    scale_factor = HEAD ** (-0.5)
    scores = (
        jnp.einsum("qhe,khe->hqk", queries, key_rows, preferred_element_type=jnp.float32)
        * scale_factor
    )
    row_max = jnp.max(scores, axis=-1, keepdims=True)
    shifted = jnp.exp(scores - row_max)
    row_total = jnp.sum(shifted, axis=-1, keepdims=True)
    exact_probability = shifted / row_total
    probability = exact_probability.astype(bfloat)
    attended = jnp.einsum("hqk,khe->qhe", probability, values, preferred_element_type=jnp.float32)
    attended = attended.reshape(length, D).astype(bfloat)
    branch = jnp.dot(attended, proj_weight, preferred_element_type=jnp.float32) + proj_bias
    middle = rows_wide + gate_one * branch
    normed_two, inverse_two = normalize_rows(middle)
    hidden_two = (normed_two * (1.0 + scale_two) + shift_two).astype(bfloat)
    pre_gelu = jnp.dot(hidden_two, fc1_weight, preferred_element_type=jnp.float32) + fc1_bias
    activated, gelu_pull = jax.vjp(
        lambda argument: jax.nn.gelu(argument, approximate=True), pre_gelu
    )
    activated = activated.astype(bfloat)
    mlp_out = jnp.dot(activated, fc2_weight, preferred_element_type=jnp.float32) + fc2_bias
    block_out = (live * (middle + gate_two * mlp_out)).astype(bfloat)

    grad_out = live * cot_rows.astype(jnp.float32)
    gate_two_grad = jnp.sum(grad_out * mlp_out, axis=0, keepdims=True)
    grad_mlp = (gate_two * grad_out).astype(bfloat)
    fc2_bias_grad = jnp.sum(grad_mlp.astype(jnp.float32), axis=0)
    grad_act = against_weight(grad_mlp, fc2_weight)
    grad_pre = gelu_pull(grad_act)[0].astype(bfloat)
    fc1_bias_grad = jnp.sum(grad_pre.astype(jnp.float32), axis=0)
    grad_hidden_two = against_weight(grad_pre, fc1_weight)
    shift_two_grad = jnp.sum(grad_hidden_two, axis=0, keepdims=True)
    scale_two_grad = jnp.sum(grad_hidden_two * normed_two, axis=0, keepdims=True)
    grad_middle = grad_out + norm_backward(
        grad_hidden_two * (1.0 + scale_two), normed_two, inverse_two
    )
    gate_one_grad = jnp.sum(grad_middle * branch, axis=0, keepdims=True)
    grad_branch = (gate_one * grad_middle).astype(bfloat)
    proj_bias_grad = jnp.sum(grad_branch.astype(jnp.float32), axis=0)
    grad_attended = (
        against_weight(grad_branch, proj_weight).astype(bfloat).reshape(length, HEADS, HEAD)
    )
    grad_prob = jnp.einsum(
        "qhe,khe->hqk", grad_attended, values, preferred_element_type=jnp.float32
    )
    inner_sum = jnp.sum(exact_probability * grad_prob, axis=-1, keepdims=True)
    grad_scores = (exact_probability * (grad_prob - inner_sum)).astype(bfloat)
    grad_queries = (
        jnp.einsum("hqk,khe->qhe", grad_scores, key_rows, preferred_element_type=jnp.float32)
        * scale_factor
    )
    grad_keys = (
        jnp.einsum("hqk,qhe->khe", grad_scores, queries, preferred_element_type=jnp.float32)
        * scale_factor
    )
    grad_values = jnp.einsum(
        "hqk,qhe->khe", probability, grad_attended, preferred_element_type=jnp.float32
    )
    grad_projected = jnp.concatenate(
        [
            grad_queries.reshape(length, D),
            grad_keys.reshape(length, D),
            grad_values.reshape(length, D),
        ],
        axis=1,
    ).astype(bfloat)
    summed = jnp.sum(grad_projected.astype(jnp.float32), axis=0)
    qv_bias_grad = jnp.concatenate([summed[:D], summed[2 * D :]])
    grad_hidden_one = against_weight(grad_projected, qkv_weight)
    shift_one_grad = jnp.sum(grad_hidden_one, axis=0, keepdims=True)
    scale_one_grad = jnp.sum(grad_hidden_one * normed_one, axis=0, keepdims=True)
    latent_grad = (
        grad_middle + norm_backward(grad_hidden_one * (1.0 + scale_one), normed_one, inverse_one)
    ).astype(bfloat)
    mod_grad = jnp.concatenate(
        [
            shift_one_grad,
            scale_one_grad,
            gate_one_grad,
            shift_two_grad,
            scale_two_grad,
            gate_two_grad,
        ],
        axis=-1,
    )
    weight_grads = (
        contract_rows(hidden_one, grad_projected).astype(bfloat),
        contract_rows(attended, grad_branch).astype(bfloat),
        contract_rows(hidden_two, grad_pre).astype(bfloat),
        contract_rows(activated, grad_mlp).astype(bfloat),
    )
    bias_grads = (qv_bias_grad, proj_bias_grad, fc1_bias_grad, fc2_bias_grad)
    return block_out, latent_grad, mod_grad, weight_grads, bias_grads


def pack_shard(qkv, proj, fc1, fc2):
    tall = fc2.shape[0] // fc1.shape[0]
    folded = fc2.reshape(tall, fc1.shape[0], fc2.shape[1]).transpose(1, 0, 2).reshape(fc1.shape)
    return jnp.concatenate([jnp.concatenate([qkv, proj], axis=1), fc1, folded], axis=0)


def unpack_shard(shard, qkv_width, low_width):
    height = shard.shape[0] // 3
    tall = shard.shape[1] // low_width
    first, second, third = shard[:height], shard[height : 2 * height], shard[2 * height :]
    folded = third.reshape(height, tall, low_width).transpose(1, 0, 2).reshape(-1, low_width)
    return first[:, :qkv_width], first[:, qkv_width:], second, folded


def unpack_full(blocks, qkv_width, low_width):
    columns, rows, height, width = blocks.shape
    height = height // 3
    tall = width // low_width

    def wide(part):
        return part.transpose(1, 2, 0, 3).reshape(rows * height, -1)

    first = blocks[:, :, :height]
    fc2 = blocks[:, :, 2 * height :].reshape(columns, rows, height, tall, low_width)
    return (
        wide(first[..., :qkv_width]),
        wide(first[..., qkv_width:]),
        wide(blocks[:, :, height : 2 * height]),
        fc2.transpose(1, 3, 2, 0, 4).reshape(rows * tall * height, columns * low_width),
    )


def pack_full(weight_grads, columns, rows):
    qkv, proj, fc1, fc2 = weight_grads
    height = qkv.shape[0] // rows

    def blocked(grad):
        return grad.reshape(rows, height, columns, -1).transpose(2, 0, 1, 3)

    tall = fc2.shape[0] // (rows * height)
    folded = fc2.reshape(rows, tall, height, columns, -1).transpose(3, 0, 2, 1, 4)
    folded = folded.reshape(columns, rows, height, -1)
    first = jnp.concatenate([blocked(qkv), blocked(proj)], axis=3)
    return jnp.concatenate([first, blocked(fc1), folded], axis=2)


def per_device(
    latents,
    conditioning,
    cotangent,
    latent_count,
    ada_weight,
    ada_bias,
    qkv_weight,
    qv_bias,
    proj_weight,
    proj_bias,
    fc1_weight,
    fc1_bias,
    fc2_weight,
    fc2_bias,
):
    rows, columns = lax.axis_size("dp"), lax.axis_size("fsdp")
    row_index = lax.axis_index("dp")
    live = latent_count[0].astype(jnp.float32)
    depth = ada_weight.shape[0]
    mod_width = ada_weight.shape[1]
    own_biases = (qv_bias, proj_bias, fc1_bias, fc2_bias)
    widths = [bias.shape[0] for bias in own_biases]
    cuts = [mod_width + sum(widths[:place]) for place in range(len(widths))]

    cond_row = conditioning.astype(jnp.float32)
    cond_act = jax.nn.silu(cond_row).astype(bfloat)
    cond_all = lax.all_gather(cond_act, ("dp", "fsdp"), axis=0, tiled=True)
    cond_owned = lax.dynamic_slice_in_dim(cond_all, row_index * depth, depth, 1)
    partial = jnp.dot(cond_owned, ada_weight, preferred_element_type=jnp.float32)
    mod_rows = lax.psum_scatter(partial, "dp", scatter_dimension=0, tiled=True)
    mod_rows = mod_rows + ada_bias.astype(jnp.float32)
    bias_row = jnp.concatenate(own_biases).astype(jnp.float32)
    payload = jnp.concatenate(
        [mod_rows, jnp.broadcast_to(bias_row, (columns, bias_row.shape[0]))], axis=1
    )
    arrived = lax.all_to_all(payload, "fsdp", split_axis=0, concat_axis=0, tiled=True)
    modulation = arrived[:, :mod_width].reshape(1, -1)
    biases = tuple(
        arrived[:, cut : cut + width].reshape(-1) for cut, width in zip(cuts, widths)
    )

    shard = pack_shard(qkv_weight, proj_weight, fc1_weight, fc2_weight)
    blocks = gather_shards(shard, rows, columns)
    weights = unpack_full(blocks, qkv_weight.shape[1], fc2_weight.shape[1])
    block_out, latent_grad, mod_grad, weight_grads, bias_grads = layer(
        latents[0], cond_act, live, cotangent[0], modulation, weights, biases
    )
    grads = pack_full(weight_grads, columns, rows)
    owned = scatter_shards(grads)
    qkv_grad, proj_grad, fc1_grad, fc2_grad = unpack_shard(
        owned, qkv_weight.shape[1], fc2_weight.shape[1]
    )

    leaving = jnp.concatenate(
        [mod_grad.reshape(columns, -1)] + [grad.reshape(columns, -1) for grad in bias_grads], axis=1
    )
    group_rows = lax.all_to_all(leaving, "fsdp", split_axis=0, concat_axis=0, tiled=True)
    all_rows = lax.all_gather(group_rows, "dp", axis=0, tiled=True)
    mod_owned = all_rows[:, :mod_width]
    ada_grad = contract_exact(cond_owned.astype(jnp.float32), mod_owned)
    sums = jnp.sum(all_rows, axis=0)
    ada_bias_grad = sums[:mod_width]
    bias_sums = [sums[cut : cut + width] for cut, width in zip(cuts, widths)]
    back = lax.dot_general(
        mod_owned, ada_weight.astype(jnp.float32), (((1,), (1,)), ((), ())), precision=highest
    )
    back = lax.psum_scatter(
        back.reshape(rows, columns, depth), "fsdp", scatter_dimension=1, tiled=True
    )
    back = lax.all_to_all(
        back.reshape(rows, depth), "dp", split_axis=0, concat_axis=0, tiled=True
    ).reshape(1, -1)
    cond_grad = jax.vjp(jax.nn.silu, cond_row)[1](back)[0]
    return (
        block_out[None],
        latent_grad[None],
        cond_grad,
        ada_grad,
        ada_bias_grad,
        qkv_grad,
        bias_sums[0],
        proj_grad,
        bias_sums[1],
        fc1_grad,
        bias_sums[2],
        fc2_grad,
        bias_sums[3],
    )


def solution(mesh):
    in_specs = (
        P(("dp", "fsdp"), None, None),
        P(("dp", "fsdp"), None),
        P(("dp", "fsdp"), None, None),
        P(("dp", "fsdp")),
        P("dp", "fsdp"),
        P("fsdp"),
        P("dp", "fsdp"),
        P("fsdp"),
        P("dp", "fsdp"),
        P("fsdp"),
        P("dp", "fsdp"),
        P("fsdp"),
        P("dp", "fsdp"),
        P("fsdp"),
    )
    out_specs = (
        P(("dp", "fsdp"), None, None),
        P(("dp", "fsdp"), None, None),
        P(("dp", "fsdp"), None),
        P("dp", "fsdp"),
        P("fsdp"),
        P("dp", "fsdp"),
        P("fsdp"),
        P("dp", "fsdp"),
        P("fsdp"),
        P("dp", "fsdp"),
        P("fsdp"),
        P("dp", "fsdp"),
        P("fsdp"),
    )
    return jax.shard_map(
        per_device, mesh=mesh, in_specs=in_specs, out_specs=out_specs, check_vma=False
    )
```

```python
import functools
import jax
import jax.numpy as jnp
from jax import lax
from jax.sharding import PartitionSpec as P
from jax.experimental import pallas as pl
from jax.experimental.pallas import tpu as pltpu

MESH_IDS = pl.DeviceIdType.MESH
D = 768
HEADS = 12
HEAD = 64
FF = 3072

highest = lax.Precision.HIGHEST
bfloat = jnp.bfloat16


def place(dp_index, z_index, core):
    return (dp_index, z_index * 2 + core)


def z_order(size):
    steps = [0]
    for distance in range(1, size // 2 + 1):
        steps.append(distance)
        if size - distance != distance:
            steps.append(size - distance)
    return steps


def enter_barrier(partners):
    barrier = pltpu.get_barrier_semaphore()
    for partner in partners:
        pl.semaphore_signal(barrier, inc=1, device_id=partner, device_id_type=MESH_IDS)
    pl.semaphore_wait(barrier, len(partners))


def positions(rows, depth):
    dp = lax.axis_index("dp")
    column = lax.axis_index("fsdp")
    z, core = column // 2, column % 2
    others = [(dp ^ 1), (dp ^ 2)] if rows == 4 else [(dp + step) % rows for step in range(1, rows)]
    partners = [place(dp, z, 1 - core)]
    partners += [place(other, z, core) for other in others]
    partners += [place(dp, (z + step) % depth, core) for step in z_order(depth)[1:]]
    return dp, z, core, others, partners


def block_of(array, line, row, shape, turned):
    if len(array.shape) == 4:
        return array.at[line, row]
    high, wide = (line, row) if turned else (row, line)
    height, width = shape
    return array.at[
        pl.ds(pl.multiple_of(high * height, height), height),
        pl.ds(pl.multiple_of(wide * width, width), width),
    ]


def whole_shape(shape, turned, rows, columns):
    height, width = shape
    if width % 128 == 0 and height % 32 == 0:
        return (columns * height, rows * width) if turned else (rows * height, columns * width)
    return (columns, rows, height, width)


def gather_kernel(rows, depth, *refs):
    shards, outs = refs[:3], refs[3:6]
    own_sems, send_sems, recv_sems = refs[6:]
    dp, z, core, others, partners = positions(rows, depth)
    sibling = place(dp, z, 1 - core)
    enter_barrier(partners)
    sends = []

    def slot_of(part, line, row):
        return block_of(outs[part], line, row, shards[part].shape, part == 2)

    def half_of(ref, part, which):
        half = shards[part].shape[0] // 2
        return ref.at[pl.ds(which * half, half)]

    def send(line, row, target, which=None, own=False):
        for part in range(3):
            destination = slot_of(part, line, row)
            source = shards[part] if own else destination
            if which is not None:
                source, destination = half_of(source, part, which), half_of(destination, part, which)
            copy = pltpu.make_async_remote_copy(
                src_ref=source,
                dst_ref=destination,
                send_sem=send_sems.at[len(sends)],
                recv_sem=recv_sems.at[which or 0, part, line, row],
                device_id=target,
                device_id_type=MESH_IDS,
            )
            copy.start()
            sends.append(copy)

    def arrive(line, row, which=None):
        for part in range(3):
            destination = slot_of(part, line, row)
            if which is not None:
                destination = half_of(destination, part, which)
            pltpu.make_async_remote_copy(
                src_ref=destination,
                dst_ref=destination,
                send_sem=send_sems.at[0],
                recv_sem=recv_sems.at[which or 0, part, line, row],
                device_id=sibling,
                device_id_type=MESH_IDS,
            ).wait_recv()

    own = z * 2 + core
    steps = z_order(depth)
    lines = [((z - step) % depth) * 2 + core for step in steps]
    for other in others:
        send(own, dp, place(other, z, core), own=True)
    for step in steps[1:]:
        send(own, dp, place(dp, (z + step) % depth, core), own=True)
    send(own, dp, sibling, own=True)
    keeps = [
        pltpu.make_async_copy(shards[part], slot_of(part, own, dp), own_sems.at[part])
        for part in range(3)
    ]
    for keep in keeps:
        keep.start()
    for turn in range(depth + 2):
        if 0 < turn < depth:
            line = lines[turn]
            arrive(line, dp)
            for other in others:
                send(line, dp, place(other, z, core))
            send(line, dp, sibling)
        if 1 <= turn <= depth:
            line = lines[turn - 1]
            for position, other in enumerate(others):
                arrive(line, other)
                if rows == 4:
                    send(line, other, place(others[1 - position], z, core), which=position)
                send(line, other, sibling)
        if turn >= 2 and rows == 4:
            line = lines[turn - 2]
            arrive(line, dp ^ 3, 0)
            arrive(line, dp ^ 3, 1)
            send(line, dp ^ 3, sibling)
    for line in lines:
        for row in range(rows):
            arrive(line + 1 - 2 * core, (dp + row) % rows)
    for keep in keeps:
        keep.wait()
    for copy in sends:
        copy.wait_send()


def gather_shards(shards, rows, columns):
    depth = columns // 2
    count = (depth - 1) + depth * rows + depth * (rows - 1) + (2 * depth if rows == 4 else 0)
    shapes = [
        whole_shape(shard.shape, part == 2, rows, columns) for part, shard in enumerate(shards)
    ]
    return pl.pallas_call(
        functools.partial(gather_kernel, rows, depth),
        out_shape=[jax.ShapeDtypeStruct(shape, bfloat) for shape in shapes],
        in_specs=[pl.BlockSpec(memory_space=pl.ANY)] * 3,
        out_specs=[pl.BlockSpec(memory_space=pl.ANY)] * 3,
        scratch_shapes=[
            pltpu.SemaphoreType.DMA((3,)),
            pltpu.SemaphoreType.DMA((3 * count,)),
            pltpu.SemaphoreType.DMA((2, 3, columns, rows)),
        ],
        compiler_params=pltpu.CompilerParams(collective_id=0, has_side_effects=True),
        name="gather_shards",
    )(*shards)


def scatter_kernel(rows, depth, *refs):
    grads, outs = refs[:3], refs[3:6]
    helds, pairs_in, planes_in, crosses_in, alongs_in = (
        refs[6 + 3 * kind : 9 + 3 * kind] for kind in range(5)
    )
    (
        load_sems, pair_send, pair_recv, plane_send, plane_recv,
        cross_send, cross_recv, along_send, along_recv,
    ) = refs[21:]
    dp, z, core, others, partners = positions(rows, depth)
    sibling = place(dp, z, 1 - core)
    targets = [dp ^ 3, dp ^ 1, dp ^ 2, dp] if rows == 4 else others + [dp]
    steps = z_order(depth)[::-1]
    enter_barrier(partners)
    waits = []

    def remote(source, destination, send_sem, recv_sem, target):
        copy = pltpu.make_async_remote_copy(
            src_ref=source, dst_ref=destination, send_sem=send_sem, recv_sem=recv_sem,
            device_id=target, device_id_type=MESH_IDS,
        )
        copy.start()
        waits.append(copy)
        return copy

    def add(first, others_in, length, target):
        chunk = 48 if length % 48 == 0 else 16

        @pl.loop(0, length // chunk)
        def _(index):
            piece = pl.ds(pl.multiple_of(index * chunk, chunk), chunk)
            total = first[piece, :].astype(jnp.float32)
            for other in others_in:
                total = total + other[piece, :].astype(jnp.float32)
            target[piece, :] = total.astype(target.dtype)

    lines = [(z + step) % depth for step in steps]
    pairs, loads, planes, crosses, alongs = {}, {}, {}, {}, {}
    for turn, line in enumerate(lines):
        for slot, target in enumerate(targets):
            for part in range(3):
                key = (part, turn, slot)
                shape = outs[part].shape
                pairs[key] = remote(
                    block_of(grads[part], line * 2 + 1 - core, target, shape, part == 2),
                    pairs_in[part].at[turn, slot], pair_send.at[key], pair_recv.at[key], sibling)
                loads[key] = pltpu.make_async_copy(
                    block_of(grads[part], line * 2 + core, target, shape, part == 2),
                    helds[part].at[turn, slot], load_sems.at[key])
                loads[key].start()
    last = len(targets) - 1
    for turn in range(depth + 2):
        if turn < depth:
            for slot in range(len(targets)):
                for part in range(3):
                    key = (part, turn, slot)
                    height = outs[part].shape[0]
                    half = height // 2
                    loads[key].wait()
                    pairs[key].wait_recv()
                    here = helds[part].at[turn, slot]
                    add(here, [pairs_in[part].at[turn, slot]], height, here)
                    if rows == 4 and slot == 0:
                        for position in range(2):
                            key = (part, turn, position)
                            crosses[key] = remote(
                                helds[part].at[turn, 0, pl.ds((1 - position) * half, half)],
                                crosses_in[part].at[turn, position],
                                cross_send.at[key], cross_recv.at[key],
                                place(others[position], z, core))
                    if rows != 4 and slot < last:
                        planes[key] = remote(
                            here, planes_in[part].at[turn, slot], plane_send.at[key],
                            plane_recv.at[key], place(targets[slot], z, core))
        if rows == 4 and 1 <= turn <= depth:
            now = turn - 1
            for position in range(2):
                for part in range(3):
                    half = outs[part].shape[0] // 2
                    crosses[part, now, 1 - position].wait_recv()
                    piece = helds[part].at[now, 1 + position, pl.ds(position * half, half)]
                    add(piece, [crosses_in[part].at[now, 1 - position]], half, piece)
                    key = (part, now, position)
                    planes[key] = remote(
                        helds[part].at[now, 1 + position], planes_in[part].at[now, position],
                        plane_send.at[key], plane_recv.at[key],
                        place(others[position], z, core))
        if turn >= 2:
            now = turn - 2
            for part in range(3):
                for slot in range(len(others)):
                    planes[part, now, slot].wait_recv()
                here = helds[part].at[now, last]
                arrived = [planes_in[part].at[now, slot] for slot in range(len(others))]
                add(here, arrived, outs[part].shape[0], here)
                if now < depth - 1:
                    key = (part, now)
                    alongs[key] = remote(
                        here, alongs_in[part].at[now], along_send.at[key], along_recv.at[key],
                        place(dp, lines[now], core))
    for part in range(3):
        for now in range(depth - 1):
            alongs[part, now].wait_recv()
        arrived = [alongs_in[part].at[now] for now in range(depth - 1)]
        add(helds[part].at[depth - 1, last], arrived, outs[part].shape[0], outs[part])
    for copy in waits:
        copy.wait_send()


def scatter_shards(grads, shapes, rows, columns):
    depth = columns // 2
    peers = 2 if rows == 4 else rows - 1
    dma = pltpu.SemaphoreType.DMA
    buffers = []
    for lead in ((depth, rows), (depth, rows), (depth, peers), (depth, 2), (depth - 1,)):
        for height, width in shapes:
            if lead == (depth, 2) and len(buffers) >= 9:
                height = height // 2 if rows == 4 else 16
            buffers.append(pltpu.VMEM(lead + (height, width), bfloat))
    return pl.pallas_call(
        functools.partial(scatter_kernel, rows, depth),
        out_shape=[jax.ShapeDtypeStruct(shape, jnp.float32) for shape in shapes],
        in_specs=[pl.BlockSpec(memory_space=pl.ANY)] * 3,
        out_specs=[pl.BlockSpec(memory_space=pltpu.VMEM)] * 3,
        scratch_shapes=buffers + [
            dma((3, depth, rows)), dma((3, depth, rows)), dma((3, depth, rows)),
            dma((3, depth, peers)), dma((3, depth, peers)),
            dma((3, depth, 2)), dma((3, depth, 2)),
            dma((3, depth - 1)), dma((3, depth - 1)),
        ],
        compiler_params=pltpu.CompilerParams(
            collective_id=1, has_side_effects=True, vmem_limit_bytes=50 * 2**20),
        name="scatter_shards",
    )(*grads)


def normalize_rows(values):
    center = jnp.mean(values, axis=-1, keepdims=True)
    spread = jnp.mean(jnp.square(values - center), axis=-1, keepdims=True)
    inverse = lax.rsqrt(spread + 1e-06)
    return ((values - center) * inverse, inverse)


def norm_backward(grad_normed, normed, inverse):
    centered = grad_normed - jnp.mean(grad_normed, axis=-1, keepdims=True)
    return inverse * (centered - normed * jnp.mean(grad_normed * normed, axis=-1, keepdims=True))


def contract_rows(left_rows, right_rows):
    return lax.dot_general(
        left_rows, right_rows, (((0,), (0,)), ((), ())), preferred_element_type=jnp.float32
    )


def contract_exact(left_rows, right_rows):
    return lax.dot_general(left_rows, right_rows, (((0,), (0,)), ((), ())), precision=highest)


def against_weight(grad_rows, weight):
    return lax.dot_general(
        grad_rows, weight, (((1,), (1,)), ((), ())), preferred_element_type=jnp.float32
    )


def pick(mixed, columns, kind):
    width = mixed.shape[1] // columns
    edge = 3 * width // 4
    low, high = (0, edge) if kind == 0 else (edge, width)
    return jnp.concatenate(
        [mixed[:, block * width + low : block * width + high] for block in range(columns)], axis=1
    )


def spread(rows_in, columns, kind):
    width = rows_in.shape[1] // columns
    rest = width // 3 if kind == 0 else 3 * width
    zeros = jnp.zeros((rows_in.shape[0], rest), rows_in.dtype)
    pieces = []
    for block in range(columns):
        piece = rows_in[:, block * width : (block + 1) * width]
        pieces += [piece, zeros] if kind == 0 else [zeros, piece]
    return jnp.concatenate(pieces, axis=1)


def layer(latent_rows, cond_act, live, cot_rows, modulation, weights, biases, columns):
    mixed_weight, fc1_weight, fc2_turned = weights
    qv_bias, proj_bias, fc1_bias, fc2_bias = biases
    length = latent_rows.shape[0]
    rows_wide = latent_rows.astype(jnp.float32)
    shift_one, scale_one, gate_one, shift_two, scale_two, gate_two = jnp.split(
        modulation, 6, axis=-1
    )
    normed_one, inverse_one = normalize_rows(rows_wide)
    hidden_one = (normed_one * (1.0 + scale_one) + shift_one).astype(bfloat)
    qkv_bias = jnp.concatenate([qv_bias[:D], jnp.zeros((D,), jnp.float32), qv_bias[D:]])
    projected = (
        pick(jnp.dot(hidden_one, mixed_weight, preferred_element_type=jnp.float32), columns, 0)
        + qkv_bias
    ).astype(bfloat)
    queries = projected[:, :D].reshape(length, HEADS, HEAD)
    key_rows = projected[:, D : 2 * D].reshape(length, HEADS, HEAD)
    values = projected[:, 2 * D :].reshape(length, HEADS, HEAD)
    scale_factor = HEAD ** (-0.5)
    scores = (
        jnp.einsum("qhe,khe->hqk", queries, key_rows, preferred_element_type=jnp.float32)
        * scale_factor
    )
    row_max = jnp.max(scores, axis=-1, keepdims=True)
    shifted = jnp.exp(scores - row_max)
    row_total = jnp.sum(shifted, axis=-1, keepdims=True)
    exact_probability = shifted / row_total
    probability = exact_probability.astype(bfloat)
    attended = jnp.einsum("hqk,khe->qhe", probability, values, preferred_element_type=jnp.float32)
    attended = attended.reshape(length, D).astype(bfloat)
    branch = pick(jnp.dot(attended, mixed_weight, preferred_element_type=jnp.float32), columns, 1)
    branch = branch + proj_bias
    middle = rows_wide + gate_one * branch
    normed_two, inverse_two = normalize_rows(middle)
    hidden_two = (normed_two * (1.0 + scale_two) + shift_two).astype(bfloat)
    pre_gelu = jnp.dot(hidden_two, fc1_weight, preferred_element_type=jnp.float32) + fc1_bias
    activated, gelu_pull = jax.vjp(
        lambda argument: jax.nn.gelu(argument, approximate=True), pre_gelu
    )
    activated = activated.astype(bfloat)
    mlp_out = against_weight(activated, fc2_turned) + fc2_bias
    block_out = (live * (middle + gate_two * mlp_out)).astype(bfloat)

    grad_out = live * cot_rows.astype(jnp.float32)
    gate_two_grad = jnp.sum(grad_out * mlp_out, axis=0, keepdims=True)
    grad_mlp = (gate_two * grad_out).astype(bfloat)
    fc2_bias_grad = jnp.sum(grad_mlp.astype(jnp.float32), axis=0)
    grad_act = jnp.dot(grad_mlp, fc2_turned, preferred_element_type=jnp.float32)
    grad_pre = gelu_pull(grad_act)[0].astype(bfloat)
    fc1_bias_grad = jnp.sum(grad_pre.astype(jnp.float32), axis=0)
    grad_hidden_two = against_weight(grad_pre, fc1_weight)
    shift_two_grad = jnp.sum(grad_hidden_two, axis=0, keepdims=True)
    scale_two_grad = jnp.sum(grad_hidden_two * normed_two, axis=0, keepdims=True)
    grad_middle = grad_out + norm_backward(
        grad_hidden_two * (1.0 + scale_two), normed_two, inverse_two
    )
    gate_one_grad = jnp.sum(grad_middle * branch, axis=0, keepdims=True)
    grad_branch = (gate_one * grad_middle).astype(bfloat)
    proj_bias_grad = jnp.sum(grad_branch.astype(jnp.float32), axis=0)
    spread_branch = spread(grad_branch, columns, 1)
    grad_attended = (
        against_weight(spread_branch, mixed_weight).astype(bfloat).reshape(length, HEADS, HEAD)
    )
    grad_prob = jnp.einsum(
        "qhe,khe->hqk", grad_attended, values, preferred_element_type=jnp.float32
    )
    inner_sum = jnp.sum(exact_probability * grad_prob, axis=-1, keepdims=True)
    grad_scores = (exact_probability * (grad_prob - inner_sum)).astype(bfloat)
    grad_queries = (
        jnp.einsum("hqk,khe->qhe", grad_scores, key_rows, preferred_element_type=jnp.float32)
        * scale_factor
    )
    grad_keys = (
        jnp.einsum("hqk,qhe->khe", grad_scores, queries, preferred_element_type=jnp.float32)
        * scale_factor
    )
    grad_values = jnp.einsum(
        "hqk,qhe->khe", probability, grad_attended, preferred_element_type=jnp.float32
    )
    grad_projected = jnp.concatenate(
        [
            grad_queries.reshape(length, D),
            grad_keys.reshape(length, D),
            grad_values.reshape(length, D),
        ],
        axis=1,
    ).astype(bfloat)
    summed = jnp.sum(grad_projected.astype(jnp.float32), axis=0)
    qv_bias_grad = jnp.concatenate([summed[:D], summed[2 * D :]])
    spread_projected = spread(grad_projected, columns, 0)
    grad_hidden_one = against_weight(spread_projected, mixed_weight)
    shift_one_grad = jnp.sum(grad_hidden_one, axis=0, keepdims=True)
    scale_one_grad = jnp.sum(grad_hidden_one * normed_one, axis=0, keepdims=True)
    latent_grad = (
        grad_middle + norm_backward(grad_hidden_one * (1.0 + scale_one), normed_one, inverse_one)
    ).astype(bfloat)
    mod_grad = jnp.concatenate(
        [
            shift_one_grad,
            scale_one_grad,
            gate_one_grad,
            shift_two_grad,
            scale_two_grad,
            gate_two_grad,
        ],
        axis=-1,
    )
    weight_grads = (
        contract_rows(
            jnp.concatenate([hidden_one, attended]),
            jnp.concatenate([spread_projected, spread_branch]),
        ).astype(bfloat),
        contract_rows(hidden_two, grad_pre).astype(bfloat),
        contract_rows(grad_mlp, activated).astype(bfloat),
    )
    bias_grads = (qv_bias_grad, proj_bias_grad, fc1_bias_grad, fc2_bias_grad)
    return block_out, latent_grad, mod_grad, weight_grads, bias_grads


def flatten_blocks(blocks, turned):
    if blocks.ndim == 2:
        return blocks
    columns, rows, height, width = blocks.shape
    if turned:
        return blocks.transpose(0, 2, 1, 3).reshape(columns * height, rows * width)
    return blocks.transpose(1, 2, 0, 3).reshape(rows * height, columns * width)


def cut_blocks(whole, shape, turned, rows, columns):
    if len(whole_shape(shape, turned, rows, columns)) == 2:
        return whole
    height, width = shape
    if turned:
        return whole.reshape(columns, height, rows, width).transpose(0, 2, 1, 3)
    return whole.reshape(rows, height, columns, width).transpose(2, 0, 1, 3)


def per_device(
    latents,
    conditioning,
    cotangent,
    latent_count,
    ada_weight,
    ada_bias,
    qkv_weight,
    qv_bias,
    proj_weight,
    proj_bias,
    fc1_weight,
    fc1_bias,
    fc2_weight,
    fc2_bias,
):
    rows, columns = lax.axis_size("dp"), lax.axis_size("fsdp")
    row_index = lax.axis_index("dp")
    live = latent_count[0].astype(jnp.float32)
    depth = ada_weight.shape[0]
    mod_width = ada_weight.shape[1]
    own_biases = (qv_bias, proj_bias, fc1_bias, fc2_bias)
    widths = [bias.shape[0] for bias in own_biases]
    cuts = [mod_width + sum(widths[:place]) for place in range(len(widths))]

    cond_row = conditioning.astype(jnp.float32)
    cond_act = jax.nn.silu(cond_row).astype(bfloat)
    cond_all = lax.all_gather(cond_act, ("dp", "fsdp"), axis=0, tiled=True)
    cond_owned = lax.dynamic_slice_in_dim(cond_all, row_index * depth, depth, 1)
    partial = jnp.dot(cond_owned, ada_weight, preferred_element_type=jnp.float32)
    mod_rows = lax.psum_scatter(partial, "dp", scatter_dimension=0, tiled=True)
    mod_rows = mod_rows + ada_bias.astype(jnp.float32)
    bias_row = jnp.concatenate(own_biases).astype(jnp.float32)
    payload = jnp.concatenate(
        [mod_rows, jnp.broadcast_to(bias_row, (columns, bias_row.shape[0]))], axis=1
    )
    arrived = lax.all_to_all(payload, "fsdp", split_axis=0, concat_axis=0, tiled=True)
    modulation = arrived[:, :mod_width].reshape(1, -1)
    biases = tuple(
        arrived[:, cut : cut + width].reshape(-1) for cut, width in zip(cuts, widths)
    )

    qkv_width = qkv_weight.shape[1]
    shards = (
        jnp.concatenate([qkv_weight, proj_weight], axis=1),
        fc1_weight,
        fc2_weight.T,
    )
    shapes = [shard.shape for shard in shards]
    blocks = gather_shards(shards, rows, columns)
    weights = [flatten_blocks(block, part == 2) for part, block in enumerate(blocks)]
    block_out, latent_grad, mod_grad, weight_grads, bias_grads = layer(
        latents[0], cond_act, live, cotangent[0], modulation, weights, biases, columns
    )
    grads = [
        cut_blocks(grad, shapes[part], part == 2, rows, columns)
        for part, grad in enumerate(weight_grads)
    ]
    mixed_grad, fc1_grad, fc2_turned_grad = scatter_shards(grads, shapes, rows, columns)
    qkv_grad, proj_grad = mixed_grad[:, :qkv_width], mixed_grad[:, qkv_width:]
    fc2_grad = fc2_turned_grad.T

    leaving = jnp.concatenate(
        [mod_grad.reshape(columns, -1)] + [grad.reshape(columns, -1) for grad in bias_grads], axis=1
    )
    group_rows = lax.all_to_all(leaving, "fsdp", split_axis=0, concat_axis=0, tiled=True)
    all_rows = lax.all_gather(group_rows, "dp", axis=0, tiled=True)
    mod_owned = all_rows[:, :mod_width]
    ada_grad = contract_exact(cond_owned.astype(jnp.float32), mod_owned)
    sums = jnp.sum(all_rows, axis=0)
    ada_bias_grad = sums[:mod_width]
    bias_sums = [sums[cut : cut + width] for cut, width in zip(cuts, widths)]
    back = lax.dot_general(
        mod_owned, ada_weight.astype(jnp.float32), (((1,), (1,)), ((), ())), precision=highest
    )
    back = lax.psum_scatter(
        back.reshape(rows, columns, depth), "fsdp", scatter_dimension=1, tiled=True
    )
    back = lax.all_to_all(
        back.reshape(rows, depth), "dp", split_axis=0, concat_axis=0, tiled=True
    ).reshape(1, -1)
    cond_grad = jax.vjp(jax.nn.silu, cond_row)[1](back)[0]
    return (
        block_out[None],
        latent_grad[None],
        cond_grad,
        ada_grad,
        ada_bias_grad,
        qkv_grad,
        bias_sums[0],
        proj_grad,
        bias_sums[1],
        fc1_grad,
        bias_sums[2],
        fc2_grad,
        bias_sums[3],
    )


def solution(mesh):
    in_specs = (
        P(("dp", "fsdp"), None, None),
        P(("dp", "fsdp"), None),
        P(("dp", "fsdp"), None, None),
        P(("dp", "fsdp")),
        P("dp", "fsdp"),
        P("fsdp"),
        P("dp", "fsdp"),
        P("fsdp"),
        P("dp", "fsdp"),
        P("fsdp"),
        P("dp", "fsdp"),
        P("fsdp"),
        P("dp", "fsdp"),
        P("fsdp"),
    )
    out_specs = (
        P(("dp", "fsdp"), None, None),
        P(("dp", "fsdp"), None, None),
        P(("dp", "fsdp"), None),
        P("dp", "fsdp"),
        P("fsdp"),
        P("dp", "fsdp"),
        P("fsdp"),
        P("dp", "fsdp"),
        P("fsdp"),
        P("dp", "fsdp"),
        P("fsdp"),
        P("dp", "fsdp"),
        P("fsdp"),
    )
    return jax.shard_map(
        per_device, mesh=mesh, in_specs=in_specs, out_specs=out_specs, check_vma=False
    )
```
